32 devices in a mesh: section: 2 (over y), ep: 16 (over z, x, core).
Axes of the slice: x: 2, y: 2, z: 4, core: 2. Of those that a mesh axis runs over, the one named last changes fastest.
Arguments:
- grad_output: bfloat16 [2, 2048, 3584], P('section', 'ep'), may hold values from -6 to 6
- route_ids: int32 [2, 2048, 2], P('section', 'ep'), may hold values from 0 to 3, all different within a row; in each aligned block of 128 rows (0 to 127, 128 to 255, ..., all dimensions but the last counted through in order) at most 80 rows name the same one
- route_gates: float32 [2, 2048, 2], P('section', 'ep'), may hold values from 0.25 to 1
- gate_pre: bfloat16 [2, 16, 16, 80, 256], P('section', 'ep'), may hold values from -6 to 6
- up_pre: bfloat16 [2, 16, 16, 80, 256], P('section', 'ep'), may hold values from -6 to 6
- w_gate: bfloat16 [2, 16, 3584, 256], P('section', 'ep'), may hold values from -0.09375 to 0.09375
- w_up: bfloat16 [2, 16, 3584, 256], P('section', 'ep'), may hold values from -0.09375 to 0.09375
- w_down: bfloat16 [2, 16, 256, 3584], P('section', 'ep'), may hold values from -0.1875 to 0.1875
Outputs:
- input_grad: bfloat16 [2, 2048, 3584], P('section', 'ep')
The draws below stay inside these ranges and needn't reach their ends.
Inputs may be any that keep to these rules, and one draw needn't show every extreme that they name: `route_ids`: in each section the 128 tokens of one index of ep name any expert at most 80 times, a bound that some block reaches; a token names 2 different experts.
All inputs are finite; a program needn't handle non-finite values.
Results may differ from the reference program's by a relative error of at most 0.0072.
Values may be sent and summed in bfloat16 or wider, within the bound.
No kernel may reach another device: no remote copies, remote signals or barrier semaphores. Data moves between devices by JAX's collectives and lax.ppermute only.
A program may use at most 128 MiB of HBM per device.

```python
import math
import jax
import jax.numpy as jnp
import numpy as np
from jax import lax

D = 3584
F_DEV = 256
SPLIT = 4
FF = 1024
TOP = 2
TOK_DEV = 128
EXPERTS = 4
CAP = 80
TOKENS = 2048
SECTIONS = 2
N_EP = 16


def levels(own_key, dims, pieces, least, top_value):
    def one(axis_at, shards_of):
        draws = jax.random.uniform(jax.random.fold_in(jax.random.fold_in(own_key, 6), axis_at), (shards_of,), jnp.float32, least / len(pieces), top_value / len(pieces))
        return jnp.repeat(jnp.exp(draws), dims[axis_at] // shards_of).reshape((-1,) + (1,) * (len(dims) - axis_at - 1))

    loudness = one(*pieces[0])
    for cut in pieces[1:]:
        loudness = loudness * one(*cut)
    return loudness


def assign_block(rng, own, number, rows, amount, top, reach, lean):
    sequence = jax.random.permutation(rng, amount)
    heavy_load, usual = portions_of(amount, rows * top, reach, lean, True), portions_of(amount, rows * top, reach, lean, False)
    places = jnp.arange(amount)

    def named(sizes, turn):
        used = int((sizes > 0).sum())
        fixed = max(1, used // 4)
        passed = fixed + (places - fixed + turn * (used - fixed)) % max(1, amount - fixed)
        return jnp.zeros((amount,), jnp.int32).at[sequence[jnp.where(places < fixed, places, passed)]].set(jnp.asarray(sizes, jnp.int32))

    sizes = jnp.where(number % 4 == 0, named(heavy_load, number // 4), named(usual, number - number // 4 - 1))
    mixed = jax.random.permutation(jax.random.fold_in(own, 3), amount)
    giver, taker = mixed[0:amount // 2 * 2:2], mixed[1:amount // 2 * 2:2]
    margin = jnp.minimum(sizes[giver] - 1, reach - sizes[taker]) // 2
    margin = jnp.where((giver == sequence[0]) | (taker == sequence[0]) | (sizes[taker] == 0), 0, jnp.maximum(margin, 0))
    passed = jax.random.randint(jax.random.fold_in(own, 4), (amount // 2,), 0, 1 << 20) % (margin + 1)
    sizes = sizes.at[giver].add(-passed).at[taker].add(passed)
    members = jnp.searchsorted(jnp.cumsum(sizes), jnp.arange(rows * top), side="right").astype(jnp.int32)
    table = members.reshape(top, rows).T
    table = table[jax.random.permutation(jax.random.fold_in(own, 1), rows)]
    turn = jax.random.randint(jax.random.fold_in(own, 2), (rows, 1), 0, top)
    return jnp.take_along_axis(table, (jnp.arange(top)[None, :] + turn) % top, axis=1)


def portions_of(count, total, most, lean, full):
    weights = [(1 << 20) // math.isqrt(standing ** lean) + 1 for standing in range(1, count + 1)]
    largest = most if full else min(most, max(-(-total // count), total * weights[0] // sum(weights)))
    least = 1 if total - largest >= count - 1 else 0
    counts, rest = [largest] + [least] * (count - 1), total - largest - least * (count - 1)
    while rest > 0:
        free = [i for i in range(1, count) if counts[i] < largest] or [i for i in range(1, count) if counts[i] < most]
        mass, budget = sum([weights[i] for i in free]), rest
        for i in free:
            addition = min(most - counts[i], max(1, budget * weights[i] // mass), rest)
            counts[i] = counts[i] + addition
            rest = rest - addition
    return np.array(counts)


def centred(stream_key, extent, deviation, most, cuts=(), kind=jnp.bfloat16):
    loudness = levels(stream_key, extent, cuts, -0.22, 0.18) if cuts else 1.0
    result = jax.random.normal(stream_key, extent, jnp.float32) * deviation * loudness
    return jnp.minimum(jnp.maximum(result, -most), most).astype(kind)


def setup_inputs(seed: int = 0) -> dict:
    seeds = jax.random.split(jax.random.key(seed), 9)
    grad_output = centred(seeds[0], (SECTIONS, TOKENS, D), 1.0, 6.0, ((0, 2), (1, 16)))
    route_ids_keys = jax.random.split(jax.random.fold_in(seeds[1], 1), SECTIONS * TOKENS // TOK_DEV)
    route_ids_turns = jax.random.permutation(jax.random.fold_in(seeds[1], 3), SECTIONS * TOKENS // TOK_DEV)
    route_ids = jax.vmap(lambda own, number: assign_block(jax.random.fold_in(seeds[1], 2), own, number, TOK_DEV, EXPERTS, TOP, CAP, 2))(route_ids_keys, route_ids_turns).reshape((SECTIONS, TOKENS, TOP))
    route_gates = jnp.clip(0.25 + 0.75 * jax.random.uniform(seeds[2], (SECTIONS, TOKENS, TOP), jnp.float32) ** levels(seeds[2], (SECTIONS, TOKENS, TOP), ((0, 2), (1, 16)), -0.2, 0.2), 0.25, 1.0)
    gate_pre = centred(seeds[3], (SECTIONS, N_EP, N_EP, CAP, F_DEV), 1.0, 6.0, ((0, 2), (1, 16)))
    up_pre = centred(seeds[4], (SECTIONS, N_EP, N_EP, CAP, F_DEV), 1.0, 6.0, ((0, 2), (1, 16)))
    w_gate = centred(seeds[5], (SECTIONS, N_EP, D, F_DEV), D ** -0.5, 0.09375, ((0, 2), (1, 16)))
    w_up = centred(seeds[6], (SECTIONS, N_EP, D, F_DEV), D ** -0.5, 0.09375, ((0, 2), (1, 16)))
    w_down = centred(seeds[7], (SECTIONS, N_EP, F_DEV, D), FF ** -0.5, 0.1875, ((0, 2), (1, 16)))
    return dict(grad_output=grad_output, route_ids=route_ids, route_gates=route_gates, gate_pre=gate_pre, up_pre=up_pre, w_gate=w_gate, w_up=w_up, w_down=w_down)


def slot_numbers(expert_list):
    onehot = (expert_list[:, None] == jnp.arange(EXPERTS, dtype=jnp.int32)[None, :]).astype(jnp.int32)
    ranks = jnp.cumsum(onehot, axis=0) - 1
    return lax.optimization_barrier(jnp.sum(onehot * ranks, axis=1)).astype(jnp.int32)

def piece_grad(routed_rows, gate_saved, up_saved, gate_matrix, up_matrix, down_matrix):
    contract = (((1,), (1,)), ((), ()))
    hidden_grad = lax.dot_general(routed_rows, down_matrix, contract, preferred_element_type=jnp.float32)
    gate_value = gate_saved.astype(jnp.float32)
    up_value = up_saved.astype(jnp.float32)
    sigma = jax.nn.sigmoid(gate_value)
    gate_grad = (hidden_grad * up_value * sigma * (1.0 + gate_value * (1.0 - sigma))).astype(jnp.bfloat16)
    up_grad = (hidden_grad * gate_value * sigma).astype(jnp.bfloat16)
    partial_sum = lax.dot_general(gate_grad, gate_matrix, contract, preferred_element_type=jnp.float32)
    partial_sum = partial_sum + lax.dot_general(up_grad, up_matrix, contract, preferred_element_type=jnp.float32)
    return partial_sum.astype(jnp.bfloat16)

def section_grad(grad_rows, expert_ids, gate_values, gate_saved, up_saved, gate_pieces, up_pieces, down_pieces):
    block_ids = expert_ids.reshape(N_EP, TOK_DEV * TOP)
    slots = jax.vmap(slot_numbers)(block_ids)
    payload = (gate_values[:, :, None] * grad_rows[:, None, :].astype(jnp.float32)).astype(jnp.bfloat16)
    payload = payload.reshape(N_EP, TOK_DEV * TOP, D)
    source = jnp.broadcast_to(jnp.arange(N_EP, dtype=jnp.int32)[:, None], (N_EP, TOK_DEV * TOP))
    routed = jnp.zeros((EXPERTS, N_EP, CAP, D), jnp.bfloat16).at[block_ids, source, slots].set(payload)

    def one_expert(expert_id):
        routed_rows = routed[expert_id].reshape(N_EP * CAP, D)
        total = jnp.zeros((N_EP * CAP, D), jnp.float32)
        for piece_slot in range(SPLIT):
            piece = expert_id * SPLIT + piece_slot
            partial_sum = piece_grad(routed_rows, gate_saved[piece].reshape(N_EP * CAP, F_DEV), up_saved[piece].reshape(N_EP * CAP, F_DEV), gate_pieces[piece], up_pieces[piece], down_pieces[piece])
            total = total + partial_sum.astype(jnp.float32)
        return total.astype(jnp.bfloat16).reshape(N_EP, CAP, D)
    combined = lax.map(one_expert, jnp.arange(EXPERTS, dtype=jnp.int32))
    picked = combined[block_ids, source, slots].astype(jnp.float32)
    return lax.optimization_barrier(jnp.sum(picked.reshape(TOKENS, TOP, D), axis=1)).astype(jnp.bfloat16)

def reference(grad_output, route_ids, route_gates, gate_pre, up_pre, w_gate, w_up, w_down):
    results = []
    for section_id in range(SECTIONS):
        results.append(section_grad(grad_output[section_id], route_ids[section_id], route_gates[section_id], gate_pre[section_id], up_pre[section_id], w_gate[section_id], w_up[section_id], w_down[section_id]))
    stacked = jnp.stack(results, axis=0)
    return jnp.roll(stacked, -1, axis=0)
```

```python
import functools

import jax
import jax.numpy as jnp
from jax import lax
from jax.experimental import pallas as pl
from jax.experimental.pallas import tpu as pltpu
from jax.sharding import PartitionSpec as P

SPLIT = 4
MIB = 1 << 20


def exchange(value, mask):
    count = lax.axis_size("ep")
    return lax.ppermute(value, "ep", [(i, i ^ mask) for i in range(count)])


def to_section_before(value, mask):
    sections, count = lax.axis_size("section"), lax.axis_size("ep")
    pairs = [
        (s * count + i, (s - 1) % sections * count + (i ^ mask))
        for s in range(sections)
        for i in range(count)
    ]
    return lax.ppermute(value, ("section", "ep"), pairs)


def column_tile(width):
    for parts in (4, 2):
        if width % (128 * parts) == 0:
            return width // parts
    return width


def fill_choices(own_ref, ids_ref, choice_ref, cap, experts):
    top, tokens = ids_ref.shape
    expert = lax.broadcasted_iota(jnp.int32, (experts, tokens), 0) ^ own_ref[0]
    named = ids_ref[0:1, :] == expert
    for k in range(1, top):
        named = named | (ids_ref[k : k + 1, :] == expert)
    member = jnp.where(named, 1.0, 0.0)
    earlier = lax.broadcasted_iota(jnp.int32, (tokens, tokens), 0) < lax.broadcasted_iota(
        jnp.int32, (tokens, tokens), 1
    )
    slots = jnp.dot(
        member.astype(jnp.bfloat16),
        jnp.where(earlier, 1.0, 0.0).astype(jnp.bfloat16),
        preferred_element_type=jnp.float32,
    )
    slots = jnp.where(named, slots, -1.0)
    place = lax.broadcasted_iota(jnp.int32, (cap, tokens), 0).astype(jnp.float32)
    for k in range(experts):
        choice_ref[k * cap : (k + 1) * cap, :] = jnp.where(
            place == slots[k : k + 1, :], 1.0, 0.0
        ).astype(choice_ref.dtype)


def dispatch_kernel(cap, experts, own_ref, ids_ref, gates_ref, rows_ref, *refs):
    outs, (choice_ref, weight_ref) = refs[:experts], refs[experts:]

    @pl.when(pl.program_id(0) == 0)
    def _():
        fill_choices(own_ref, ids_ref, choice_ref, cap, experts)
        top, tokens = ids_ref.shape
        for k in range(experts):
            expert = own_ref[0] ^ k
            gate = jnp.zeros((1, tokens), jnp.float32)
            for j in range(top):
                gate = jnp.where(ids_ref[j : j + 1, :] == expert, gates_ref[j : j + 1, :], gate)
            chosen = choice_ref[k * cap : (k + 1) * cap, :].astype(jnp.float32)
            weight_ref[k * cap : (k + 1) * cap, :] = jnp.sum(chosen * gate, axis=1, keepdims=True)

    picked = jnp.dot(choice_ref[...], rows_ref[...], preferred_element_type=jnp.float32)
    payload = (picked * weight_ref[...]).astype(jnp.bfloat16)
    for k in range(experts):
        outs[k][...] = payload[k * cap : (k + 1) * cap, :]


def dispatch(own, ids, gates, rows, cap, experts):
    tokens, width = rows.shape
    tile = column_tile(width)
    whole = pl.BlockSpec(ids.shape, lambda i, own: (0, 0))
    return pl.pallas_call(
        functools.partial(dispatch_kernel, cap, experts),
        grid_spec=pltpu.PrefetchScalarGridSpec(
            num_scalar_prefetch=1,
            grid=(width // tile,),
            in_specs=[whole, whole, pl.BlockSpec((tokens, tile), lambda i, own: (0, i))],
            out_specs=[pl.BlockSpec((cap, tile), lambda i, own: (0, i))] * experts,
            scratch_shapes=[
                pltpu.VMEM((experts * cap, tokens), jnp.bfloat16),
                pltpu.VMEM((experts * cap, 1), jnp.float32),
            ],
        ),
        out_shape=[jax.ShapeDtypeStruct((cap, width), jnp.bfloat16)] * experts,
        compiler_params=pltpu.CompilerParams(vmem_limit_bytes=16 * MIB),
        cost_estimate=pl.CostEstimate(
            flops=2 * experts * cap * tokens * width, bytes_accessed=4 * MIB, transcendentals=0
        ),
        name="dispatch",
    )(own, ids, gates, rows)


def combine_kernel(cap, experts, own_ref, ids_ref, *refs):
    rows, out_ref, choice_ref = refs[:experts], refs[experts], refs[experts + 1]

    @pl.when(pl.program_id(0) == 0)
    def _():
        fill_choices(own_ref, ids_ref, choice_ref, cap, experts)

    total = None
    for k in range(experts):
        part = lax.dot_general(
            choice_ref[k * cap : (k + 1) * cap, :],
            rows[k][...],
            (((0,), (0,)), ((), ())),
            preferred_element_type=jnp.float32,
        )
        total = part if total is None else total + part
    out_ref[...] = total.astype(jnp.bfloat16)


def combine(own, ids, returned, cap, experts):
    width, tokens = returned[0].shape[1], ids.shape[1]
    tile = column_tile(width)
    return pl.pallas_call(
        functools.partial(combine_kernel, cap, experts),
        grid_spec=pltpu.PrefetchScalarGridSpec(
            num_scalar_prefetch=1,
            grid=(width // tile,),
            in_specs=[pl.BlockSpec(ids.shape, lambda i, own: (0, 0))]
            + [pl.BlockSpec((cap, tile), lambda i, own: (0, i))] * experts,
            out_specs=pl.BlockSpec((tokens, tile), lambda i, own: (0, i)),
            scratch_shapes=[pltpu.VMEM((experts * cap, tokens), jnp.bfloat16)],
        ),
        out_shape=jax.ShapeDtypeStruct((tokens, width), jnp.bfloat16),
        compiler_params=pltpu.CompilerParams(vmem_limit_bytes=16 * MIB),
        cost_estimate=pl.CostEstimate(
            flops=2 * experts * cap * tokens * width, bytes_accessed=4 * MIB, transcendentals=0
        ),
        name="combine",
    )(own, ids, *returned)


def pieces_kernel(parts, source_ref, *refs):
    blocks = refs[:SPLIT]
    gate_ref, up_ref, w_gate_ref, w_up_ref, w_down_ref = refs[SPLIT : SPLIT + 5]
    outs = refs[SPLIT + 5 : 2 * SPLIT + 5]
    rows, gates, ups, w_gate, w_up, w_down, result, row_sem, act_sem, down_sem, up_sem, out_sem = refs[
        2 * SPLIT + 5 :
    ]
    cap, width = blocks[0].shape
    hidden = w_down.shape[0]
    tile = width // parts

    def columns(i):
        return pl.ds(i * tile, tile)

    row_copies, down_copies, act_copies, weight_copies = [], [], [], []
    for i in range(parts):
        down_copies.append(
            pltpu.make_async_copy(
                w_down_ref.at[:, columns(i)], w_down.at[:, columns(i)], down_sem.at[i]
            )
        )
        for j in range(SPLIT):
            row_copies.append(
                pltpu.make_async_copy(
                    blocks[j].at[:, columns(i)],
                    rows.at[pl.ds(j * cap, cap), columns(i)],
                    row_sem.at[i, j],
                )
            )
    for j in range(SPLIT):
        at = pl.ds(j * cap, cap)
        act_copies.append(
            pltpu.make_async_copy(gate_ref.at[source_ref[j]], gates.at[at], act_sem.at[0, j])
        )
        act_copies.append(
            pltpu.make_async_copy(up_ref.at[source_ref[j]], ups.at[at], act_sem.at[1, j])
        )
    for i in range(parts):
        weight_copies.append(
            pltpu.make_async_copy(w_gate_ref.at[columns(i)], w_gate.at[columns(i)], up_sem.at[0, i])
        )
        weight_copies.append(
            pltpu.make_async_copy(w_up_ref.at[columns(i)], w_up.at[columns(i)], up_sem.at[1, i])
        )
    for copy in [*row_copies, *down_copies, *act_copies, *weight_copies]:
        copy.start()
    across = (((1,), (1,)), ((), ()))
    total = jnp.zeros((SPLIT * cap, hidden), jnp.float32)
    for i in range(parts):
        down_copies[i].wait()
        for j in range(SPLIT):
            row_copies[i * SPLIT + j].wait()
        total = total + lax.dot_general(
            rows[:, columns(i)], w_down[:, columns(i)], across, preferred_element_type=jnp.float32
        )
    for copy in act_copies:
        copy.wait()
    g = gates[...].astype(jnp.float32)
    u = ups[...].astype(jnp.float32)
    s = jax.nn.sigmoid(g)
    gate_grad = (total * u * s * (1.0 + g * (1.0 - s))).astype(jnp.bfloat16)
    up_grad = (total * g * s).astype(jnp.bfloat16)
    out_copies = []
    for i in range(parts):
        weight_copies[2 * i].wait()
        weight_copies[2 * i + 1].wait()
        part = lax.dot_general(
            gate_grad, w_gate[columns(i), :], across, preferred_element_type=jnp.float32
        )
        part = part + lax.dot_general(
            up_grad, w_up[columns(i), :], across, preferred_element_type=jnp.float32
        )
        result[:, columns(i)] = part.astype(jnp.bfloat16)
        for j in range(SPLIT):
            copy = pltpu.make_async_copy(
                result.at[pl.ds(j * cap, cap), columns(i)],
                outs[j].at[:, columns(i)],
                out_sem.at[i, j],
            )
            copy.start()
            out_copies.append(copy)
    for copy in out_copies:
        copy.wait()


def pieces(source, blocks, gate_pre, up_pre, w_gate, w_up, w_down):
    cap, width = blocks[0].shape
    hidden = w_down.shape[0]
    parts = width // column_tile(width)
    anywhere = pl.BlockSpec(memory_space=pl.ANY)
    rows = SPLIT * cap
    return pl.pallas_call(
        functools.partial(pieces_kernel, parts),
        in_specs=[pl.BlockSpec(memory_space=pltpu.SMEM)] + [anywhere] * (SPLIT + 5),
        out_specs=[anywhere] * SPLIT,
        out_shape=[jax.ShapeDtypeStruct((cap, width), jnp.bfloat16)] * SPLIT,
        scratch_shapes=[
            pltpu.VMEM((rows, width), jnp.bfloat16),
            pltpu.VMEM((rows, hidden), jnp.bfloat16),
            pltpu.VMEM((rows, hidden), jnp.bfloat16),
            pltpu.VMEM((width, hidden), jnp.bfloat16),
            pltpu.VMEM((width, hidden), jnp.bfloat16),
            pltpu.VMEM((hidden, width), jnp.bfloat16),
            pltpu.VMEM((rows, width), jnp.bfloat16),
            pltpu.SemaphoreType.DMA((parts, SPLIT)),
            pltpu.SemaphoreType.DMA((2, SPLIT)),
            pltpu.SemaphoreType.DMA((parts,)),
            pltpu.SemaphoreType.DMA((2, parts)),
            pltpu.SemaphoreType.DMA((parts, SPLIT)),
        ],
        compiler_params=pltpu.CompilerParams(vmem_limit_bytes=24 * MIB),
        cost_estimate=pl.CostEstimate(
            flops=6 * rows * width * hidden, bytes_accessed=12 * MIB, transcendentals=rows * hidden
        ),
        name="pieces",
    )(source, *blocks, gate_pre, up_pre, w_gate, w_up, w_down)


def added(a, b):
    return (a.astype(jnp.float32) + b.astype(jnp.float32)).astype(jnp.bfloat16)


def local(grad_output, route_ids, route_gates, gate_pre, up_pre, w_gate, w_up, w_down):
    experts = lax.axis_size("ep") // SPLIT
    me = lax.axis_index("ep")
    own, seat = me // SPLIT, me % SPLIT
    cap = gate_pre.shape[3]
    gate_saved, up_saved = gate_pre[0, 0], up_pre[0, 0]
    spare = -cap % 16
    if spare:
        gate_saved = jnp.pad(gate_saved, ((0, 0), (0, spare), (0, 0)))
        up_saved = jnp.pad(up_saved, ((0, 0), (0, spare), (0, 0)))
        cap += spare
    ids = route_ids[0].T
    own = own.astype(jnp.int32).reshape(1)
    ids_after = to_section_before(ids, 0)
    outgoing = dispatch(own, ids, route_gates[0].T, grad_output[0], cap, experts)
    returned = []
    for k in range(experts):
        mine = exchange(outgoing[k], k * SPLIT) if k else outgoing[k]
        far = exchange(mine, 2)
        blocks = [mine, exchange(mine, 1), far, exchange(far, 1)]
        source = ((own ^ k) * SPLIT + (seat ^ jnp.arange(SPLIT, dtype=jnp.int32))).astype(jnp.int32)
        partial = pieces(source, blocks, gate_saved, up_saved, w_gate[0, 0], w_up[0, 0], w_down[0, 0])
        near_sum = added(partial[0], exchange(partial[1], 1))
        far_sum = added(partial[2], exchange(partial[3], 1))
        whole_sum = added(near_sum, exchange(far_sum, 2))
        returned.append(to_section_before(whole_sum, k * SPLIT))
    return combine(own, ids_after, returned, cap, experts)[None]


def solution(mesh):
    placed = (
        P("section", "ep", None),
        P("section", "ep", None),
        P("section", "ep", None),
        P("section", "ep", None, None, None),
        P("section", "ep", None, None, None),
        P("section", "ep", None, None),
        P("section", "ep", None, None),
        P("section", "ep", None, None),
    )
    return jax.shard_map(
        local, mesh=mesh, in_specs=placed, out_specs=P("section", "ep", None), check_vma=False
    )
```

```python
import functools

import jax
import jax.numpy as jnp
from jax import lax
from jax.experimental import pallas as pl
from jax.experimental.pallas import tpu as pltpu
from jax.sharding import PartitionSpec as P

SPLIT = 4
MIB = 1 << 20


TIES = {
    ("plane", 3): [("plane", 2), ("pieces", 0)],
    ("chip", 2): [("pieces", 0)],
    ("chip", 1): [("pieces", 0)],
    ("chip", 3): [("pieces", 2)],
    ("pieces", 1): [("pieces", 2)],
}


def cut(experts, cap):
    return [(k, 0, cap) for k in range(experts)]


GIVEN = {
    "chip": ("plane",),
    "pieces": ("plane", "chip"),
    "chip_back": ("pieces",),
    "plane_back": ("pieces", "chip_back"),
}


def exchange(value, mask):
    count = lax.axis_size("ep")
    return lax.ppermute(value, "ep", [(i, i ^ mask) for i in range(count)])


def to_section_before(value, mask):
    sections, count = lax.axis_size("section"), lax.axis_size("ep")
    pairs = [
        (s * count + i, (s - 1) % sections * count + (i ^ mask))
        for s in range(sections)
        for i in range(count)
    ]
    return lax.ppermute(value, ("section", "ep"), pairs)


def column_tile(width):
    for parts in (4, 2):
        if width % (128 * parts) == 0:
            return width // parts
    return width


def fill_choices(own_ref, ids_ref, choice_ref, cap, experts):
    top, tokens = ids_ref.shape
    expert = lax.broadcasted_iota(jnp.int32, (experts, tokens), 0) ^ own_ref[0]
    named = ids_ref[0:1, :] == expert
    for k in range(1, top):
        named = named | (ids_ref[k : k + 1, :] == expert)
    member = jnp.where(named, 1.0, 0.0)
    earlier = lax.broadcasted_iota(jnp.int32, (tokens, tokens), 0) < lax.broadcasted_iota(
        jnp.int32, (tokens, tokens), 1
    )
    slots = jnp.dot(
        member.astype(jnp.bfloat16),
        jnp.where(earlier, 1.0, 0.0).astype(jnp.bfloat16),
        preferred_element_type=jnp.float32,
    )
    slots = jnp.where(named, slots, -1.0)
    place = lax.broadcasted_iota(jnp.int32, (cap, tokens), 0).astype(jnp.float32)
    for k in range(experts):
        choice_ref[k * cap : (k + 1) * cap, :] = jnp.where(
            place == slots[k : k + 1, :], 1.0, 0.0
        ).astype(choice_ref.dtype)


def dispatch_kernel(cap, experts, units, own_ref, ids_ref, gates_ref, rows_ref, *refs):
    outs, (choice_ref, weight_ref) = refs[: len(units)], refs[len(units) :]

    @pl.when(pl.program_id(0) == 0)
    def _():
        fill_choices(own_ref, ids_ref, choice_ref, cap, experts)
        top, tokens = ids_ref.shape
        for k in range(experts):
            expert = own_ref[0] ^ k
            gate = jnp.zeros((1, tokens), jnp.float32)
            for j in range(top):
                gate = jnp.where(ids_ref[j : j + 1, :] == expert, gates_ref[j : j + 1, :], gate)
            chosen = choice_ref[k * cap : (k + 1) * cap, :].astype(jnp.float32)
            weight_ref[k * cap : (k + 1) * cap, :] = jnp.sum(chosen * gate, axis=1, keepdims=True)

    picked = jnp.dot(choice_ref[...], rows_ref[...], preferred_element_type=jnp.float32)
    payload = (picked * weight_ref[...]).astype(jnp.bfloat16)
    for out_ref, (k, first, count) in zip(outs, units):
        out_ref[...] = payload[k * cap + first : k * cap + first + count, :]


def dispatch(own, ids, gates, rows, cap, experts, units):
    tokens, width = rows.shape
    tile = column_tile(width)
    whole = pl.BlockSpec(ids.shape, lambda i, own: (0, 0))
    return pl.pallas_call(
        functools.partial(dispatch_kernel, cap, experts, units),
        grid_spec=pltpu.PrefetchScalarGridSpec(
            num_scalar_prefetch=1,
            grid=(width // tile,),
            in_specs=[whole, whole, pl.BlockSpec((tokens, tile), lambda i, own: (0, i))],
            out_specs=[pl.BlockSpec((count, tile), lambda i, own: (0, i)) for _, _, count in units],
            scratch_shapes=[
                pltpu.VMEM((experts * cap, tokens), jnp.bfloat16),
                pltpu.VMEM((experts * cap, 1), jnp.float32),
            ],
        ),
        out_shape=[jax.ShapeDtypeStruct((count, width), jnp.bfloat16) for _, _, count in units],
        compiler_params=pltpu.CompilerParams(vmem_limit_bytes=16 * MIB),
        cost_estimate=pl.CostEstimate(
            flops=1000, bytes_accessed=1000, transcendentals=0
        ),
        name="dispatch",
    )(own, ids, gates, rows)


def combine_kernel(cap, experts, units, own_ref, ids_ref, *refs):
    rows, out_ref, choice_ref = refs[: len(units)], refs[-2], refs[-1]

    @pl.when(pl.program_id(0) == 0)
    def _():
        fill_choices(own_ref, ids_ref, choice_ref, cap, experts)

    total = None
    for rows_ref, (k, first, count) in zip(rows, units):
        part = lax.dot_general(
            choice_ref[k * cap + first : k * cap + first + count, :],
            rows_ref[...],
            (((0,), (0,)), ((), ())),
            preferred_element_type=jnp.float32,
        )
        total = part if total is None else total + part
    out_ref[...] = total.astype(jnp.bfloat16)


def combine(own, ids, returned, cap, experts, units):
    width, tokens = returned[0].shape[1], ids.shape[1]
    tile = column_tile(width)
    return pl.pallas_call(
        functools.partial(combine_kernel, cap, experts, units),
        grid_spec=pltpu.PrefetchScalarGridSpec(
            num_scalar_prefetch=1,
            grid=(width // tile,),
            in_specs=[pl.BlockSpec(ids.shape, lambda i, own: (0, 0))]
            + [pl.BlockSpec((count, tile), lambda i, own: (0, i)) for _, _, count in units],
            out_specs=pl.BlockSpec((tokens, tile), lambda i, own: (0, i)),
            scratch_shapes=[pltpu.VMEM((experts * cap, tokens), jnp.bfloat16)],
        ),
        out_shape=jax.ShapeDtypeStruct((tokens, width), jnp.bfloat16),
        compiler_params=pltpu.CompilerParams(vmem_limit_bytes=16 * MIB),
        cost_estimate=pl.CostEstimate(
            flops=1000, bytes_accessed=1000, transcendentals=0
        ),
        name="combine",
    )(own, ids, *returned)


def pieces_kernel(parts, first, source_ref, *refs):
    blocks, saved, weights, outs = refs[:2], refs[2:6], refs[6:12], refs[12:14]
    here, sem = refs[14:]
    count, width = blocks[0].shape
    tile = width // parts
    copies = []
    for n, ref in enumerate(saved):
        for j in range(2):
            copies.append(
                pltpu.make_async_copy(
                    ref.at[source_ref[n // 2, j], pl.ds(first, count)],
                    here.at[n, pl.ds(j * count, count)],
                    sem.at[n, j],
                )
            )
    for copy in copies:
        copy.start()
    across = (((1,), (1,)), ((), ()))
    rows = jnp.concatenate([block[...] for block in blocks], axis=0)
    totals = [
        lax.dot_general(rows, weights[3 * n + 2][...], across, preferred_element_type=jnp.float32)
        for n in range(2)
    ]
    for copy in copies:
        copy.wait()
    grads = []
    for n in range(2):
        g = here[2 * n].astype(jnp.float32)
        u = here[2 * n + 1].astype(jnp.float32)
        s = jax.nn.sigmoid(g)
        grads.append((totals[n] * u * s * (1.0 + g * (1.0 - s))).astype(jnp.bfloat16))
        grads.append((totals[n] * g * s).astype(jnp.bfloat16))
    for i in range(parts):
        at = pl.ds(i * tile, tile)
        part = None
        for grad, weight in zip(grads, (weights[0], weights[1], weights[3], weights[4])):
            term = lax.dot_general(grad, weight[at, :], across, preferred_element_type=jnp.float32)
            part = term if part is None else part + term
        part = part.astype(jnp.bfloat16)
        for j in range(2):
            outs[j][:, at] = part[j * count : (j + 1) * count, :]


def pieces(first, source, blocks, saved, weights):
    count, width = blocks[0].shape
    hidden = weights[2].shape[0]
    parts = width // 512 if width % 512 == 0 else 1
    anywhere = pl.BlockSpec(memory_space=pl.ANY)
    near = pl.BlockSpec(memory_space=pltpu.VMEM)
    return pl.pallas_call(
        functools.partial(pieces_kernel, parts, first),
        in_specs=[pl.BlockSpec(memory_space=pltpu.SMEM)] + [near] * 2 + [anywhere] * 4 + [near] * 6,
        out_specs=[near] * 2,
        out_shape=[jax.ShapeDtypeStruct((count, width), jnp.bfloat16)] * 2,
        scratch_shapes=[
            pltpu.VMEM((4, 2 * count, hidden), jnp.bfloat16),
            pltpu.SemaphoreType.DMA((4, 2)),
        ],
        compiler_params=pltpu.CompilerParams(vmem_limit_bytes=20 * MIB),
        cost_estimate=pl.CostEstimate(flops=1000, bytes_accessed=1000, transcendentals=0),
        name="pieces",
    )(source, *blocks, *saved, *weights)


def after(value, *others):
    if isinstance(value, (list, tuple)):
        return list(lax.optimization_barrier((tuple(value), *others))[0])
    return lax.optimization_barrier((value, *others))[0]


def first_of(value):
    return value[0] if isinstance(value, (list, tuple)) else value


def added(a, b):
    return (a.astype(jnp.float32) + b.astype(jnp.float32)).astype(jnp.bfloat16)


def local(grad_output, route_ids, route_gates, gate_pre, up_pre, w_gate, w_up, w_down):
    experts = lax.axis_size("ep") // SPLIT
    me = lax.axis_index("ep")
    own, seat = me // SPLIT, me % SPLIT
    cap = gate_pre.shape[3]
    gate_saved, up_saved = gate_pre[0, 0], up_pre[0, 0]
    spare = -cap % 16
    if spare:
        gate_saved = jnp.pad(gate_saved, ((0, 0), (0, spare), (0, 0)))
        up_saved = jnp.pad(up_saved, ((0, 0), (0, spare), (0, 0)))
        cap += spare
    ids = route_ids[0].T
    own = own.astype(jnp.int32).reshape(1)
    units = cut(experts, cap)
    outgoing = dispatch(own, ids, route_gates[0].T, grad_output[0], cap, experts, units)
    weights = [w_gate[0, 0], w_up[0, 0], w_down[0, 0]]
    weights = weights + [exchange(w, 1) for w in weights]
    values = {}

    def step(kind, i):
        if (kind, i) not in values:
            k, first, _ = units[i]
            given = [step(name, i) for name in GIVEN[kind]] if kind != "plane" else [outgoing[i]]
            ties = [first_of(step(*t)) for t in TIES.get((kind, i), ()) if t[1] < len(units)]
            if ties:
                given[0] = after(given[0], *ties)
            if (kind, i) == ("pieces", 0):
                given[0] = after(given[0], ids_after)
            with jax.named_scope(f"{kind}_{i}"):
                values[kind, i] = work(kind, k, first, given)
        return values[kind, i]

    def work(kind, k, first, given):
        if kind == "plane":
            return exchange(given[0], k * SPLIT) if k else given[0]
        if kind == "chip":
            return exchange(given[0], 2)
        if kind == "pieces":
            source = ((own ^ k) * SPLIT + (seat ^ jnp.array([0, 2], jnp.int32))).astype(jnp.int32)
            return pieces(first, jnp.stack([source, source // 2]), given, saved, weights)
        if kind == "chip_back":
            return exchange(given[0][1], 2)
        return to_section_before(added(given[0][0], given[1]), k * SPLIT)

    with jax.named_scope("ids"):
        ids_after = to_section_before(after(ids, outgoing[0]), 0)
    other_core = [
        lax.dynamic_index_in_dim(
            v.reshape(experts * SPLIT // 2, 2, *v.shape[1:]), 1 - seat % 2, 1, keepdims=False
        )
        for v in (after(gate_saved, outgoing[0]), after(up_saved, outgoing[0]))
    ]
    saved = [gate_saved, up_saved] + [exchange(v, 1) for v in other_core]
    returned = [step("plane_back", i) for i in range(len(units))]
    return combine(own, ids_after, returned, cap, experts, units)[None]


def solution(mesh):
    placed = (
        P("section", "ep", None),
        P("section", "ep", None),
        P("section", "ep", None),
        P("section", "ep", None, None, None),
        P("section", "ep", None, None, None),
        P("section", "ep", None, None),
        P("section", "ep", None, None),
        P("section", "ep", None, None),
    )
    return jax.shard_map(
        local, mesh=mesh, in_specs=placed, out_specs=P("section", "ep", None), check_vma=False
    )
```

```python
import functools

import jax
import jax.numpy as jnp
from jax import lax
from jax.experimental import pallas as pl
from jax.experimental.pallas import tpu as pltpu
from jax.sharding import PartitionSpec as P

SPLIT = 4
MIB = 1 << 20
IDS_AT = 1


TIES = {
    ("plane", 3): [("plane", 2)],
    ("chip", 1): [("chip_back", 0), ("pieces", 0), ("plane_back", 0)],
    ("chip", 3): [("pieces", 2)],
    ("chip_back", 1): [("plane_back", 2)],
    ("chip_back", 0): [("chip", 2)],
}


def cut(experts, cap):
    return [(k, 0, cap) for k in range(experts)]


GIVEN = {
    "chip": ("plane",),
    "pieces": ("plane", "chip"),
    "chip_back": ("pieces",),
    "plane_back": ("pieces", "chip_back"),
}


def exchange(value, mask):
    count = lax.axis_size("ep")
    return lax.ppermute(value, "ep", [(i, i ^ mask) for i in range(count)])


def to_section_before(value, mask):
    sections, count = lax.axis_size("section"), lax.axis_size("ep")
    pairs = [
        (s * count + i, (s - 1) % sections * count + (i ^ mask))
        for s in range(sections)
        for i in range(count)
    ]
    return lax.ppermute(value, ("section", "ep"), pairs)


def column_tile(width):
    for parts in (4, 2):
        if width % (128 * parts) == 0:
            return width // parts
    return width


def fill_choices(own_ref, ids_ref, choice_ref, cap, experts):
    top, tokens = ids_ref.shape
    expert = lax.broadcasted_iota(jnp.int32, (experts, tokens), 0) ^ own_ref[0]
    named = ids_ref[0:1, :] == expert
    for k in range(1, top):
        named = named | (ids_ref[k : k + 1, :] == expert)
    member = jnp.where(named, 1.0, 0.0)
    earlier = lax.broadcasted_iota(jnp.int32, (tokens, tokens), 0) < lax.broadcasted_iota(
        jnp.int32, (tokens, tokens), 1
    )
    slots = jnp.dot(
        member.astype(jnp.bfloat16),
        jnp.where(earlier, 1.0, 0.0).astype(jnp.bfloat16),
        preferred_element_type=jnp.float32,
    )
    slots = jnp.where(named, slots, -1.0)
    place = lax.broadcasted_iota(jnp.int32, (cap, tokens), 0).astype(jnp.float32)
    for k in range(experts):
        choice_ref[k * cap : (k + 1) * cap, :] = jnp.where(
            place == slots[k : k + 1, :], 1.0, 0.0
        ).astype(choice_ref.dtype)


def dispatch_kernel(cap, experts, units, own_ref, ids_ref, gates_ref, rows_ref, *refs):
    outs, (choice_ref, weight_ref) = refs[: len(units)], refs[len(units) :]

    @pl.when(pl.program_id(0) == 0)
    def _():
        fill_choices(own_ref, ids_ref, choice_ref, cap, experts)
        top, tokens = ids_ref.shape
        for k in range(experts):
            expert = own_ref[0] ^ k
            gate = jnp.zeros((1, tokens), jnp.float32)
            for j in range(top):
                gate = jnp.where(ids_ref[j : j + 1, :] == expert, gates_ref[j : j + 1, :], gate)
            chosen = choice_ref[k * cap : (k + 1) * cap, :].astype(jnp.float32)
            weight_ref[k * cap : (k + 1) * cap, :] = jnp.sum(chosen * gate, axis=1, keepdims=True)

    picked = jnp.dot(choice_ref[...], rows_ref[...], preferred_element_type=jnp.float32)
    payload = (picked * weight_ref[...]).astype(jnp.bfloat16)
    for out_ref, (k, first, count) in zip(outs, units):
        out_ref[...] = payload[k * cap + first : k * cap + first + count, :]


def dispatch(own, ids, gates, rows, cap, experts, units):
    tokens, width = rows.shape
    tile = column_tile(width)
    whole = pl.BlockSpec(ids.shape, lambda i, own: (0, 0))
    return pl.pallas_call(
        functools.partial(dispatch_kernel, cap, experts, units),
        grid_spec=pltpu.PrefetchScalarGridSpec(
            num_scalar_prefetch=1,
            grid=(width // tile,),
            in_specs=[whole, whole, pl.BlockSpec((tokens, tile), lambda i, own: (0, i))],
            out_specs=[pl.BlockSpec((count, tile), lambda i, own: (0, i)) for _, _, count in units],
            scratch_shapes=[
                pltpu.VMEM((experts * cap, tokens), jnp.bfloat16),
                pltpu.VMEM((experts * cap, 1), jnp.float32),
            ],
        ),
        out_shape=[jax.ShapeDtypeStruct((count, width), jnp.bfloat16) for _, _, count in units],
        compiler_params=pltpu.CompilerParams(vmem_limit_bytes=58 * MIB),
        cost_estimate=pl.CostEstimate(
            flops=1000, bytes_accessed=1000, transcendentals=0
        ),
        name="dispatch",
    )(own, ids, gates, rows)


def combine_kernel(cap, experts, units, own_ref, ids_ref, *refs):
    rows, out_ref, choice_ref = refs[: len(units)], refs[-2], refs[-1]

    @pl.when(pl.program_id(0) == 0)
    def _():
        fill_choices(own_ref, ids_ref, choice_ref, cap, experts)

    total = None
    for rows_ref, (k, first, count) in zip(rows, units):
        part = lax.dot_general(
            choice_ref[k * cap + first : k * cap + first + count, :],
            rows_ref[...],
            (((0,), (0,)), ((), ())),
            preferred_element_type=jnp.float32,
        )
        total = part if total is None else total + part
    out_ref[...] = total.astype(jnp.bfloat16)


def combine(own, ids, returned, cap, experts, units):
    width, tokens = returned[0].shape[1], ids.shape[1]
    tile = column_tile(width)
    return pl.pallas_call(
        functools.partial(combine_kernel, cap, experts, units),
        grid_spec=pltpu.PrefetchScalarGridSpec(
            num_scalar_prefetch=1,
            grid=(width // tile,),
            in_specs=[pl.BlockSpec(ids.shape, lambda i, own: (0, 0))]
            + [pl.BlockSpec((count, tile), lambda i, own: (0, i)) for _, _, count in units],
            out_specs=pl.BlockSpec((tokens, tile), lambda i, own: (0, i)),
            scratch_shapes=[pltpu.VMEM((experts * cap, tokens), jnp.bfloat16)],
        ),
        out_shape=jax.ShapeDtypeStruct((tokens, width), jnp.bfloat16),
        compiler_params=pltpu.CompilerParams(vmem_limit_bytes=16 * MIB),
        cost_estimate=pl.CostEstimate(
            flops=1000, bytes_accessed=1000, transcendentals=0
        ),
        name="combine",
    )(own, ids, *returned)


def pieces_kernel(parts, first, source_ref, *refs):
    blocks, saved, weights, outs = refs[:2], refs[2:6], refs[6:12], refs[12:14]
    here, sem = refs[14:]
    count, width = blocks[0].shape
    tile = width // parts
    copies = []
    for n, ref in enumerate(saved):
        for j in range(2):
            copies.append(
                pltpu.make_async_copy(
                    ref.at[source_ref[j], pl.ds(first, count)],
                    here.at[n, pl.ds(j * count, count)],
                    sem.at[n, j],
                )
            )
    for copy in copies:
        copy.start()
    across = (((1,), (1,)), ((), ()))
    rows = jnp.concatenate([block[...] for block in blocks], axis=0)
    totals = [
        lax.dot_general(rows, weights[3 * n + 2][...], across, preferred_element_type=jnp.float32)
        for n in range(2)
    ]
    for copy in copies:
        copy.wait()
    grads = []
    for n in range(2):
        g = here[2 * n].astype(jnp.float32)
        u = here[2 * n + 1].astype(jnp.float32)
        s = jax.nn.sigmoid(g)
        grads.append((totals[n] * u * s * (1.0 + g * (1.0 - s))).astype(jnp.bfloat16))
        grads.append((totals[n] * g * s).astype(jnp.bfloat16))
    for i in range(parts):
        at = pl.ds(i * tile, tile)
        part = None
        for grad, weight in zip(grads, (weights[0], weights[1], weights[3], weights[4])):
            term = lax.dot_general(grad, weight[at, :], across, preferred_element_type=jnp.float32)
            part = term if part is None else part + term
        part = part.astype(jnp.bfloat16)
        for j in range(2):
            outs[j][:, at] = part[j * count : (j + 1) * count, :]


def pieces(first, source, blocks, saved, weights):
    count, width = blocks[0].shape
    hidden = weights[2].shape[0]
    parts = width // 512 if width % 512 == 0 else 1
    anywhere = pl.BlockSpec(memory_space=pl.ANY)
    near = pl.BlockSpec(memory_space=pltpu.VMEM)
    return pl.pallas_call(
        functools.partial(pieces_kernel, parts, first),
        in_specs=[pl.BlockSpec(memory_space=pltpu.SMEM)] + [near] * 2 + [anywhere] * 4 + [near] * 6,
        out_specs=[near] * 2,
        out_shape=[jax.ShapeDtypeStruct((count, width), jnp.bfloat16)] * 2,
        scratch_shapes=[
            pltpu.VMEM((4, 2 * count, hidden), jnp.bfloat16),
            pltpu.SemaphoreType.DMA((4, 2)),
        ],
        compiler_params=pltpu.CompilerParams(vmem_limit_bytes=20 * MIB),
        cost_estimate=pl.CostEstimate(flops=1000, bytes_accessed=1000, transcendentals=0),
        name="pieces",
    )(source, *blocks, *saved, *weights)


def after(value, *others):
    if isinstance(value, (list, tuple)):
        return list(lax.optimization_barrier((tuple(value), *others))[0])
    return lax.optimization_barrier((value, *others))[0]


def first_of(value):
    return value[0] if isinstance(value, (list, tuple)) else value


def added(a, b):
    return (a.astype(jnp.float32) + b.astype(jnp.float32)).astype(jnp.bfloat16)


def local(grad_output, route_ids, route_gates, gate_pre, up_pre, w_gate, w_up, w_down):
    experts = lax.axis_size("ep") // SPLIT
    me = lax.axis_index("ep")
    own, seat = me // SPLIT, me % SPLIT
    cap = gate_pre.shape[3]
    gate_saved, up_saved = gate_pre[0, 0], up_pre[0, 0]
    spare = -cap % 16
    if spare:
        gate_saved = jnp.pad(gate_saved, ((0, 0), (0, spare), (0, 0)))
        up_saved = jnp.pad(up_saved, ((0, 0), (0, spare), (0, 0)))
        cap += spare
    ids = route_ids[0].T
    own = own.astype(jnp.int32).reshape(1)
    units = cut(experts, cap)
    outgoing = dispatch(own, ids, route_gates[0].T, grad_output[0], cap, experts, units)
    weights = [w_gate[0, 0], w_up[0, 0], w_down[0, 0]]
    weights = weights + [exchange(w, 1) for w in weights]
    values = {}

    def step(kind, i):
        if (kind, i) not in values:
            k, first, _ = units[i]
            given = [step(name, i) for name in GIVEN[kind]] if kind != "plane" else [outgoing[i]]
            ties = [first_of(step(*t)) for t in TIES.get((kind, i), ()) if t[1] < len(units)]
            mine = own
            if kind == "pieces":
                if i == IDS_AT:
                    ties.append(ids_after)
                if ties:
                    mine = after(own, *ties)
            elif ties:
                given[0] = after(given[0], *ties)
            with jax.named_scope(f"{kind}_{i}"):
                values[kind, i] = work(kind, k, first, given, mine)
        return values[kind, i]

    def work(kind, k, first, given, mine):
        if kind == "plane":
            return exchange(given[0], k * SPLIT) if k else given[0]
        if kind == "chip":
            return exchange(given[0], 2)
        if kind == "pieces":
            source = ((mine ^ k) * SPLIT + (seat ^ jnp.array([0, 2], jnp.int32))).astype(jnp.int32)
            return pieces(first, source, given, saved, weights)
        if kind == "chip_back":
            return exchange(given[0][1], 2)
        return to_section_before(added(given[0][0], given[1]), k * SPLIT)

    ids_after = to_section_before(ids, 0)
    saved = [gate_saved, up_saved, exchange(gate_saved, 1), exchange(up_saved, 1)]
    returned = [step("plane_back", i) for i in range(len(units))]
    return combine(own, ids_after, returned, cap, experts, units)[None]


def solution(mesh):
    placed = (
        P("section", "ep", None),
        P("section", "ep", None),
        P("section", "ep", None),
        P("section", "ep", None, None, None),
        P("section", "ep", None, None, None),
        P("section", "ep", None, None),
        P("section", "ep", None, None),
        P("section", "ep", None, None),
    )
    return jax.shard_map(
        local, mesh=mesh, in_specs=placed, out_specs=P("section", "ep", None), check_vma=False
    )
```

```python
import functools

import jax
import jax.numpy as jnp
from jax import lax
from jax.experimental import pallas as pl
from jax.experimental.pallas import tpu as pltpu
from jax.sharding import PartitionSpec as P

SPLIT = 4
MIB = 1 << 20
IDS_AT = 1
COSTS = (1000, 1000, 100000000000, 100000000000)


TIES = {
    ("plane", 4): [("plane", 3)],
    ("chip", 1): [("chip_back", 0)],
    ("chip", 4): [("pieces", 2)],
    ("chip_back", 1): [("plane_back", 3)],
    ("chip_back", 2): [("plane_back", 3)],
    ("chip_back", 0): [("chip", 3)],
    ("plane_back", 4): [("pieces", 1)],
}


def cut(experts, cap):
    head = -(-cap // 32) * 16
    units = []
    for k in range(experts):
        if k == 1:
            units += [(k, 0, head), (k, head, cap - head)]
        else:
            units.append((k, 0, cap))
    return units


def exchange(value, mask):
    count = lax.axis_size("ep")
    return lax.ppermute(value, "ep", [(i, i ^ mask) for i in range(count)])


def to_section_before(value, mask):
    sections, count = lax.axis_size("section"), lax.axis_size("ep")
    pairs = [
        (s * count + i, (s - 1) % sections * count + (i ^ mask))
        for s in range(sections)
        for i in range(count)
    ]
    return lax.ppermute(value, ("section", "ep"), pairs)


def column_tile(width):
    for parts in (4, 2):
        if width % (128 * parts) == 0:
            return width // parts
    return width


def fill_choices(own_ref, ids_ref, choice_ref, cap, experts):
    top, tokens = ids_ref.shape
    expert = lax.broadcasted_iota(jnp.int32, (experts, tokens), 0) ^ own_ref[0]
    named = ids_ref[0:1, :] == expert
    for k in range(1, top):
        named = named | (ids_ref[k : k + 1, :] == expert)
    member = jnp.where(named, 1.0, 0.0)
    earlier = lax.broadcasted_iota(jnp.int32, (tokens, tokens), 0) < lax.broadcasted_iota(
        jnp.int32, (tokens, tokens), 1
    )
    slots = jnp.dot(
        member.astype(jnp.bfloat16),
        jnp.where(earlier, 1.0, 0.0).astype(jnp.bfloat16),
        preferred_element_type=jnp.float32,
    )
    slots = jnp.where(named, slots, -1.0)
    place = lax.broadcasted_iota(jnp.int32, (cap, tokens), 0).astype(jnp.float32)
    for k in range(experts):
        choice_ref[k * cap : (k + 1) * cap, :] = jnp.where(
            place == slots[k : k + 1, :], 1.0, 0.0
        ).astype(choice_ref.dtype)


def dispatch_kernel(cap, experts, units, own_ref, ids_ref, gates_ref, rows_ref, *refs):
    outs, (choice_ref, weight_ref) = refs[: len(units)], refs[len(units) :]

    @pl.when(pl.program_id(0) == 0)
    def _():
        fill_choices(own_ref, ids_ref, choice_ref, cap, experts)
        top, tokens = ids_ref.shape
        for k in range(experts):
            expert = own_ref[0] ^ k
            gate = jnp.zeros((1, tokens), jnp.float32)
            for j in range(top):
                gate = jnp.where(ids_ref[j : j + 1, :] == expert, gates_ref[j : j + 1, :], gate)
            chosen = choice_ref[k * cap : (k + 1) * cap, :].astype(jnp.float32)
            weight_ref[k * cap : (k + 1) * cap, :] = jnp.sum(chosen * gate, axis=1, keepdims=True)

    picked = jnp.dot(choice_ref[...], rows_ref[...], preferred_element_type=jnp.float32)
    payload = (picked * weight_ref[...]).astype(jnp.bfloat16)
    for out_ref, (k, first, count) in zip(outs, units):
        out_ref[...] = payload[k * cap + first : k * cap + first + count, :]


def dispatch(own, ids, gates, rows, cap, experts, units):
    tokens, width = rows.shape
    tile = column_tile(width)
    whole = pl.BlockSpec(ids.shape, lambda i, own: (0, 0))
    return pl.pallas_call(
        functools.partial(dispatch_kernel, cap, experts, units),
        grid_spec=pltpu.PrefetchScalarGridSpec(
            num_scalar_prefetch=1,
            grid=(width // tile,),
            in_specs=[whole, whole, pl.BlockSpec((tokens, tile), lambda i, own: (0, i))],
            out_specs=[pl.BlockSpec((count, tile), lambda i, own: (0, i)) for _, _, count in units],
            scratch_shapes=[
                pltpu.VMEM((experts * cap, tokens), jnp.bfloat16),
                pltpu.VMEM((experts * cap, 1), jnp.float32),
            ],
        ),
        out_shape=[jax.ShapeDtypeStruct((count, width), jnp.bfloat16) for _, _, count in units],
        compiler_params=pltpu.CompilerParams(vmem_limit_bytes=58 * MIB),
        cost_estimate=pl.CostEstimate(
            flops=1000, bytes_accessed=1000, transcendentals=0
        ),
        name="dispatch",
    )(own, ids, gates, rows)


def combine_kernel(cap, experts, units, own_ref, ids_ref, *refs):
    rows, out_ref, choice_ref = refs[: len(units)], refs[-2], refs[-1]

    @pl.when(pl.program_id(0) == 0)
    def _():
        fill_choices(own_ref, ids_ref, choice_ref, cap, experts)

    total = None
    for rows_ref, (k, first, count) in zip(rows, units):
        part = lax.dot_general(
            choice_ref[k * cap + first : k * cap + first + count, :],
            rows_ref[...],
            (((0,), (0,)), ((), ())),
            preferred_element_type=jnp.float32,
        )
        total = part if total is None else total + part
    out_ref[...] = total.astype(jnp.bfloat16)


def combine(own, ids, returned, cap, experts, units):
    width, tokens = returned[0].shape[1], ids.shape[1]
    tile = column_tile(width)
    return pl.pallas_call(
        functools.partial(combine_kernel, cap, experts, units),
        grid_spec=pltpu.PrefetchScalarGridSpec(
            num_scalar_prefetch=1,
            grid=(width // tile,),
            in_specs=[pl.BlockSpec(ids.shape, lambda i, own: (0, 0))]
            + [pl.BlockSpec((count, tile), lambda i, own: (0, i)) for _, _, count in units],
            out_specs=pl.BlockSpec((tokens, tile), lambda i, own: (0, i)),
            scratch_shapes=[pltpu.VMEM((experts * cap, tokens), jnp.bfloat16)],
        ),
        out_shape=jax.ShapeDtypeStruct((tokens, width), jnp.bfloat16),
        compiler_params=pltpu.CompilerParams(vmem_limit_bytes=16 * MIB),
        cost_estimate=pl.CostEstimate(
            flops=1000, bytes_accessed=1000, transcendentals=0
        ),
        name="combine",
    )(own, ids, *returned)


def pieces_kernel(parts, spans, source_ref, *refs):
    blocks, refs = refs[: 2 * len(spans)], refs[2 * len(spans) :]
    saved, weights, refs = refs[:4], refs[4:10], refs[10:]
    outs, (here, sem) = refs[:-2], refs[-2:]
    width = blocks[0].shape[1]
    tile = width // parts
    places, at = [], 0
    for j in range(2):
        for first, count in spans:
            places.append((j, first, count, at))
            at += count
    copies = []
    for n, ref in enumerate(saved):
        for i, (j, first, count, at) in enumerate(places):
            copies.append(
                pltpu.make_async_copy(
                    ref.at[source_ref[j], pl.ds(first, count)],
                    here.at[n, pl.ds(at, count)],
                    sem.at[n, i],
                )
            )
    for copy in copies:
        copy.start()
    across = (((1,), (1,)), ((), ()))
    rows = jnp.concatenate([block[...] for block in blocks], axis=0)
    totals = [
        lax.dot_general(rows, weights[3 * n + 2][...], across, preferred_element_type=jnp.float32)
        for n in range(2)
    ]
    for copy in copies:
        copy.wait()
    grads = []
    for n in range(2):
        g = here[2 * n].astype(jnp.float32)
        u = here[2 * n + 1].astype(jnp.float32)
        s = jax.nn.sigmoid(g)
        grads.append((totals[n] * u * s * (1.0 + g * (1.0 - s))).astype(jnp.bfloat16))
        grads.append((totals[n] * g * s).astype(jnp.bfloat16))
    for i in range(parts):
        columns = pl.ds(i * tile, tile)
        part = None
        for grad, weight in zip(grads, (weights[0], weights[1], weights[3], weights[4])):
            term = lax.dot_general(
                grad, weight[columns, :], across, preferred_element_type=jnp.float32
            )
            part = term if part is None else part + term
        part = part.astype(jnp.bfloat16)
        for out_ref, (_, _, count, at) in zip(outs, places):
            out_ref[:, columns] = part[at : at + count, :]


def pieces(cost, spans, source, blocks, saved, weights):
    width = blocks[0].shape[1]
    hidden = weights[2].shape[0]
    parts = width // 512 if width % 512 == 0 else 1
    rows = sum(block.shape[0] for block in blocks)
    anywhere = pl.BlockSpec(memory_space=pl.ANY)
    near = pl.BlockSpec(memory_space=pltpu.VMEM)
    return pl.pallas_call(
        functools.partial(pieces_kernel, parts, spans),
        in_specs=[pl.BlockSpec(memory_space=pltpu.SMEM)]
        + [near] * len(blocks)
        + [anywhere] * 4
        + [near] * 6,
        out_specs=[near] * len(blocks),
        out_shape=[jax.ShapeDtypeStruct(block.shape, jnp.bfloat16) for block in blocks],
        scratch_shapes=[
            pltpu.VMEM((4, rows, hidden), jnp.bfloat16),
            pltpu.SemaphoreType.DMA((4, len(blocks))),
        ],
        compiler_params=pltpu.CompilerParams(vmem_limit_bytes=20 * MIB),
        cost_estimate=pl.CostEstimate(flops=cost, bytes_accessed=1000, transcendentals=0),
        name="pieces",
    )(source, *blocks, *saved, *weights)


def after(value, *others):
    if isinstance(value, (list, tuple)):
        return list(lax.optimization_barrier((tuple(value), *others))[0])
    return lax.optimization_barrier((value, *others))[0]


def first_of(value):
    return value[0] if isinstance(value, (list, tuple)) else value


def added(a, b):
    return (a.astype(jnp.float32) + b.astype(jnp.float32)).astype(jnp.bfloat16)


def local(grad_output, route_ids, route_gates, gate_pre, up_pre, w_gate, w_up, w_down):
    experts = lax.axis_size("ep") // SPLIT
    me = lax.axis_index("ep")
    own, seat = me // SPLIT, me % SPLIT
    cap = gate_pre.shape[3]
    gate_saved, up_saved = gate_pre[0, 0], up_pre[0, 0]
    spare = -cap % 16
    if spare:
        gate_saved = jnp.pad(gate_saved, ((0, 0), (0, spare), (0, 0)))
        up_saved = jnp.pad(up_saved, ((0, 0), (0, spare), (0, 0)))
        cap += spare
    ids = route_ids[0].T
    own = own.astype(jnp.int32).reshape(1)
    units = cut(experts, cap)
    outgoing = dispatch(own, ids, route_gates[0].T, grad_output[0], cap, experts, units)
    weights = [w_gate[0, 0], w_up[0, 0], w_down[0, 0]]
    weights = weights + [exchange(w, 1) for w in weights]
    values = {}

    def parts_of(k):
        return [j for j, unit in enumerate(units) if unit[0] == k]

    def step(kind, i):
        if (kind, i) not in values:
            if kind == "pieces":
                given = [step(name, j) for name in ("plane", "chip") for j in parts_of(i)]
            elif kind == "plane":
                given = [outgoing[i]]
            elif kind == "chip":
                given = [step("plane", i)]
            else:
                mine = parts_of(units[i][0])
                rows = step("pieces", units[i][0])
                at = mine.index(i)
                given = [rows[at], rows[len(mine) + at]]
                given = given[1:] if kind == "chip_back" else [given[0], step("chip_back", i)]
            ties = [first_of(step(*t)) for t in TIES.get((kind, i), ()) if t[1] < len(units)]
            with jax.named_scope(f"{kind}_{i}"):
                values[kind, i] = work(kind, i, given, ties)
        return values[kind, i]

    def work(kind, i, given, ties):
        if kind == "pieces":
            ties = ties + [ids_after] * (i == IDS_AT)
            mine = after(own, *ties) if ties else own
            source = ((mine ^ i) * SPLIT + (seat ^ jnp.array([0, 2], jnp.int32))).astype(jnp.int32)
            return pieces(COSTS[i % len(COSTS)], [units[j][1:] for j in parts_of(i)], source, given, saved, weights)
        if ties:
            given[0] = after(given[0], *ties)
        k = units[i][0]
        if kind == "plane":
            return exchange(given[0], k * SPLIT) if k else given[0]
        if kind in ("chip", "chip_back"):
            return exchange(given[0], 2)
        return to_section_before(added(*given), k * SPLIT)

    ids_after = to_section_before(ids, 0)
    saved = [gate_saved, up_saved, exchange(gate_saved, 1), exchange(up_saved, 1)]
    returned = [step("plane_back", i) for i in range(len(units))]
    return combine(own, ids_after, returned, cap, experts, units)[None]


def solution(mesh):
    placed = (
        P("section", "ep", None),
        P("section", "ep", None),
        P("section", "ep", None),
        P("section", "ep", None, None, None),
        P("section", "ep", None, None, None),
        P("section", "ep", None, None),
        P("section", "ep", None, None),
        P("section", "ep", None, None),
    )
    return jax.shard_map(
        local, mesh=mesh, in_specs=placed, out_specs=P("section", "ep", None), check_vma=False
    )
```
